512 devices in a mesh: rep: 64 (over z, x_lo, core), tp: 8 (over y, x_hi).
Axes of the slice: x: 4 (x_hi: 2, x_lo: 2; x = x_hi * 2 + x_lo), y: 4, z: 16, core: 2. Of those that a mesh axis runs over, the one named last changes fastest.
Arguments:
- owner: int32 [8], replicated, may hold values from 0 to 63
- queries: bfloat16 [16384, 8192], P('rep', 'tp'), may hold values from -128 to 128
- rotated_suffix_keys: bfloat16 [16384, 1024], P('rep', 'tp'), may hold values from -16 to 16
- suffix_values: bfloat16 [16384, 1024], P('rep', 'tp'), may hold values from -6 to 6
- prefix_keys: bfloat16 [262144, 1024], P('rep', 'tp'), may hold values from -6 to 6
- prefix_values: bfloat16 [262144, 1024], P('rep', 'tp'), may hold values from -6 to 6
Outputs:
- context: bfloat16 [16384, 8192], P(('rep', 'tp'))
The draws below stay inside these ranges and needn't reach their ends.
Inputs may be any that keep to these rules, and one draw needn't show every extreme that they name: `owner`: entry k is the replica whose rows of prefix_keys and prefix_values hold key and value head k of the prompt's cache.
All inputs are finite; a program needn't handle non-finite values.
Results may differ from the reference program's by a relative error of at most 0.0046.
Values may be sent and summed in bfloat16 or wider, within the bound.
No kernel may reach another device: no remote copies, remote signals or barrier semaphores. Data moves between devices by JAX's collectives and lax.ppermute only.
A program may use at most 64 MiB of HBM per device.

```python
import jax
import jax.numpy as jnp
from jax import lax

Q_HEADS = 64
KEY_VALUE_HEADS = 8
HEAD_WIDTH = 128
PREFIX = 4096
SUFFIX_TOKENS = 256
BLOCK = 512
TOKENS = 16384
CACHE_ROWS = 262144
N_REP = 64


def suffix_base(key):
    return 2.0 * jax.random.normal(jax.random.fold_in(key, 7), (TOKENS, KEY_VALUE_HEADS * HEAD_WIDTH), jnp.float32)


def draw_rotated_suffix_keys(key, part):
    base = suffix_base(key)
    attention_output = 0.5 * base
    return attention_output.astype(jnp.bfloat16)


def draw_queries(key, part):
    key = jax.random.fold_in(key, 5)
    attention_output = jax.random.normal(key, (TOKENS, Q_HEADS * HEAD_WIDTH), jnp.float32)
    return attention_output.astype(jnp.bfloat16)


def with_ends(array, own_key, smallest, high):
    place = [jax.random.randint(jax.random.fold_in(own_key, axis), (), 0, length) for axis, length in enumerate(array.shape)]
    widest = array.shape.index(max(array.shape))
    neighbour = place[:widest] + [(place[widest] + 1) % array.shape[widest]] + place[widest + 1:]
    return array.at[tuple(place)].set(smallest).at[tuple(neighbour)].set(high)


def block_scale(own_key, extent, split, smallest, high):
    def one(dim, shards_of):
        draws = jax.random.uniform(jax.random.fold_in(jax.random.fold_in(own_key, 6), dim), (shards_of,), jnp.float32, smallest / len(split), high / len(split))
        return jnp.repeat(jnp.exp(draws), extent[dim] // shards_of).reshape((-1,) + (1,) * (len(extent) - dim - 1))

    level = one(*split[0])
    for cut in split[1:]:
        level = level * one(*cut)
    return level


def noise(own_key, extent, spread, reach, cuts=(), kind=jnp.bfloat16):
    drawn = jax.random.normal(own_key, extent, jnp.float32) * spread
    if len(cuts) > 0:
        drawn = block_scale(own_key, extent, cuts, -0.22, 0.18) * drawn
    return jnp.clip(drawn, min=-reach, max=reach).astype(kind)


def setup_inputs(seed: int = 0) -> dict:
    keys = jax.random.split(jax.random.key(seed), 7)
    owner = with_ends(jax.random.randint(keys[0], (KEY_VALUE_HEADS,), 0, N_REP), jax.random.fold_in(keys[0], 1), 0, N_REP - 1).astype(jnp.int32)
    queries = draw_queries(jax.random.fold_in(keys[6], 71), 0)
    rotated_suffix_keys = draw_rotated_suffix_keys(jax.random.fold_in(keys[6], 71), 0)
    suffix_values = noise(keys[3], (TOKENS, KEY_VALUE_HEADS * HEAD_WIDTH), 1.0, 6.0, ((0, 64), (1, 8)))
    prefix_keys = noise(keys[4], (CACHE_ROWS, KEY_VALUE_HEADS * HEAD_WIDTH), 1.0, 6.0, ((0, 64), (1, 8)))
    prefix_values = noise(keys[5], (CACHE_ROWS, KEY_VALUE_HEADS * HEAD_WIDTH), 1.0, 6.0, ((0, 64), (1, 8)))
    return dict(owner=owner, queries=queries, rotated_suffix_keys=rotated_suffix_keys, suffix_values=suffix_values, prefix_keys=prefix_keys, prefix_values=prefix_values)


def block_partials(query_matrix, key_rows, value_rows, allowed, rescale_factor):
    scores = jnp.einsum("ikgd,nkd->kgin", query_matrix.astype(jnp.float32), key_rows.astype(jnp.float32)) * rescale_factor
    scores = jnp.where(allowed, scores, jnp.float32(-1e30))
    largest = jnp.max(scores, axis=-1)
    weights = jnp.exp(scores - largest[..., None]).astype(jnp.bfloat16)
    total = jnp.sum(weights.astype(jnp.float32), axis=-1)
    partial_out = jnp.einsum("kgin,nkd->kgid", weights.astype(jnp.float32), value_rows.astype(jnp.float32))
    return largest, total, partial_out


def combine_partials(running_state, largest, total, partial_out):
    running_max, running_total, running_out = running_state
    newest = jnp.maximum(running_max, largest)
    old_factor = jnp.exp(running_max - newest)
    new_factor = jnp.exp(largest - newest)
    return (newest, running_total * old_factor + total * new_factor,
            running_out * old_factor[..., None] + partial_out * new_factor[..., None])


def owned_rows(source, owner):
    pieces = []
    for head_index in range(KEY_VALUE_HEADS):
        columns = source[:, head_index * HEAD_WIDTH:(head_index + 1) * HEAD_WIDTH]
        start_row = owner[head_index].astype(jnp.int32) * PREFIX
        pieces.append(lax.dynamic_slice_in_dim(columns, start_row, PREFIX, 0))
    return jnp.stack(pieces, axis=1)


def reference(owner, queries, rotated_suffix_keys, suffix_values, prefix_keys, prefix_values):
    group = Q_HEADS // KEY_VALUE_HEADS
    rescale_factor = 1.0 / (HEAD_WIDTH ** 0.5)
    cache_keys = owned_rows(prefix_keys, owner)
    cache_values = owned_rows(prefix_values, owner)
    query_every_head = queries.reshape(N_REP, SUFFIX_TOKENS, KEY_VALUE_HEADS, group, HEAD_WIDTH)
    suffix_key_heads = rotated_suffix_keys.reshape(N_REP, SUFFIX_TOKENS, KEY_VALUE_HEADS, HEAD_WIDTH)
    suffix_value_heads = suffix_values.reshape(N_REP, SUFFIX_TOKENS, KEY_VALUE_HEADS, HEAD_WIDTH)
    causal_mask = jnp.arange(SUFFIX_TOKENS)[None, :] <= jnp.arange(SUFFIX_TOKENS)[:, None]

    def single_replica(input_arrays):
        query_matrix, suffix_key_matrix, suffix_value_matrix = input_arrays
        running_state = (jnp.full((KEY_VALUE_HEADS, group, SUFFIX_TOKENS), -1e30, jnp.float32),
                   jnp.zeros((KEY_VALUE_HEADS, group, SUFFIX_TOKENS), jnp.float32),
                   jnp.zeros((KEY_VALUE_HEADS, group, SUFFIX_TOKENS, HEAD_WIDTH), jnp.float32))
        running_state = combine_partials(running_state, *block_partials(query_matrix, suffix_key_matrix, suffix_value_matrix, causal_mask, rescale_factor))
        everything = jnp.ones((SUFFIX_TOKENS, BLOCK), dtype=bool)

        def step_block(block_index, state):
            begin = (block_index * BLOCK).astype(jnp.int32)
            key_rows = lax.dynamic_slice_in_dim(cache_keys, begin, BLOCK, 0)
            value_rows = lax.dynamic_slice_in_dim(cache_values, begin, BLOCK, 0)
            return combine_partials(state, *block_partials(query_matrix, key_rows, value_rows, everything, rescale_factor))

        running_state = lax.fori_loop(0, PREFIX // BLOCK, step_block, running_state)
        output = running_state[2] / running_state[1][..., None]
        return jnp.transpose(output, (2, 0, 1, 3)).reshape(SUFFIX_TOKENS, Q_HEADS * HEAD_WIDTH).astype(jnp.bfloat16)

    attention_output = lax.map(single_replica, (query_every_head, suffix_key_heads, suffix_value_heads))
    return attention_output.reshape(TOKENS, Q_HEADS * HEAD_WIDTH)
```

```python
import functools
import math

import jax
import jax.numpy as jnp
from jax import lax
from jax.experimental import pallas as pl
from jax.experimental.pallas import tpu as pltpu
from jax.sharding import PartitionSpec as P

Q_HEADS = 64
KEY_VALUE_HEADS = 8
GROUP = Q_HEADS // KEY_VALUE_HEADS
WIDTH = 128
PIECE = 64
SCORE_SCALE = math.log2(math.e) / math.sqrt(WIDTH)
NEGATIVE = -1e30
LARGE = 1e30
HEADS_STEP = 2
NT = (((1,), (1,)), ((), ()))
f32, bf16 = jnp.float32, jnp.bfloat16


def with_ones(values):
    return jnp.concatenate([values, jnp.ones(values.shape, values.dtype)], axis=1)


def spread(column, count):
    return jnp.concatenate([column] * count, axis=1)


def flat(kv, part):
    return kv[:, part].reshape(kv.shape[0] * kv.shape[2], WIDTH)


def suffix_scores(query, keys):
    scores = lax.dot_general(query, keys, NT, preferred_element_type=f32) * SCORE_SCALE
    row = lax.broadcasted_iota(jnp.int32, scores.shape, 0)
    col = lax.broadcasted_iota(jnp.int32, scores.shape, 1)
    return jnp.where(col <= row, scores, NEGATIVE)


def add_piece(query, shift, kv_ref, total, tile):
    keys, values = flat(kv_ref, 0), with_ones(flat(kv_ref, 1))
    wide = spread(shift, tile // WIDTH)
    for start in range(0, keys.shape[0], tile):
        scores = lax.dot_general(query, keys[start:start + tile], NT, preferred_element_type=f32)
        weights = jnp.exp2(scores * SCORE_SCALE - wide).astype(bf16)
        total = total + jnp.dot(weights, values[start:start + tile], preferred_element_type=f32)
    return total


def first_kernel(q_ref, k_ref, v_ref, kv_ref, shift_ref, total_ref):
    for head in range(HEADS_STEP):
        query = q_ref[:, head * WIDTH:(head + 1) * WIDTH]
        scores = suffix_scores(query, k_ref[...])
        largest = jnp.max(scores, axis=1, keepdims=True)
        shift = jnp.broadcast_to(largest, (scores.shape[0], WIDTH))
        weights = jnp.exp2(scores - spread(shift, scores.shape[1] // WIDTH)).astype(bf16)
        total = jnp.dot(weights, with_ones(v_ref[...]), preferred_element_type=f32)
        shift_ref[head] = shift
        total_ref[head] = add_piece(query, shift, kv_ref, total, 512)


def next_kernel(q_ref, shift_ref, total_in, kv_ref, total_ref):
    for head in range(HEADS_STEP):
        query = q_ref[:, head * WIDTH:(head + 1) * WIDTH]
        total_ref[head] = add_piece(query, shift_ref[head], kv_ref, total_in[head], 512)


def last_kernel(q_ref, shift_ref, total_in, kv_ref, k_ref, v_ref, a_ref, b_ref, c_ref, out_ref):
    worst = []
    for head in range(HEADS_STEP):
        query = q_ref[:, head * WIDTH:(head + 1) * WIDTH]
        total = add_piece(query, shift_ref[head], kv_ref, total_in[head], 512)
        weight = total[:, WIDTH:]
        worst.append(jnp.where(weight < LARGE, 0.0, 1.0))
        out_ref[:, head * WIDTH:(head + 1) * WIDTH] = (total[:, :WIDTH] / weight).astype(bf16)

    @pl.when(jnp.max(sum(worst)) > 0.0)
    def _():
        for head in range(HEADS_STEP):
            query = q_ref[:, head * WIDTH:(head + 1) * WIDTH]
            state = (jnp.full((query.shape[0], 1), NEGATIVE, f32), jnp.zeros((query.shape[0], 2 * WIDTH), f32))

            def block(state, scores, values):
                shift, total = state
                newest = jnp.maximum(shift, jnp.max(scores, axis=1, keepdims=True))
                weights = jnp.exp2(scores - newest).astype(bf16)
                added = jnp.dot(weights, with_ones(values), preferred_element_type=f32)
                return newest, total * jnp.exp2(shift - newest) + added

            state = block(state, suffix_scores(query, k_ref[...]), v_ref[...])
            for ref in (a_ref, b_ref, c_ref, kv_ref):
                def step(i, state, ref=ref):
                    at = pl.ds(i * 4, 4)
                    keys = ref[at, 0].reshape(4 * PIECE, WIDTH)
                    values = ref[at, 1].reshape(4 * PIECE, WIDTH)
                    scores = lax.dot_general(query, keys, NT, preferred_element_type=f32) * SCORE_SCALE
                    return block(state, scores, values)
                state = lax.fori_loop(0, ref.shape[0] // 4, step, state)
            total = state[1]
            out_ref[:, head * WIDTH:(head + 1) * WIDTH] = (total[:, :WIDTH] / total[:, WIDTH:]).astype(bf16)


def whole(array):
    return pl.BlockSpec(array.shape, lambda i: (0,) * array.ndim)


def call(kernel, queries, others, out_shapes, out_specs, specs, keys):
    flops = 4 * queries.shape[0] * GROUP * keys * WIDTH
    return pl.pallas_call(
        kernel,
        grid=(GROUP // HEADS_STEP,),
        in_specs=[pl.BlockSpec((queries.shape[0], HEADS_STEP * WIDTH), lambda i: (0, i))] + specs,
        out_specs=out_specs,
        out_shape=out_shapes,
        compiler_params=pltpu.CompilerParams(vmem_limit_bytes=48 * 1024 * 1024),
        cost_estimate=pl.CostEstimate(flops=3 * flops, bytes_accessed=4 * 1024 * 1024, transcendentals=0),
    )(queries, *others)


def local(owner, queries, rotated_suffix_keys, suffix_values, prefix_keys, prefix_values):
    rep, tp = lax.axis_index("rep"), lax.axis_index("tp")
    size = lax.axis_size("rep")
    rows = queries.shape[0]
    mine = owner[tp]
    core, side = rep % 2, (rep // 2) % 2
    owner_core, owner_side, owner_z = mine % 2, (mine // 2) % 2, mine // 4
    swap_core = [(i, i ^ 1) for i in range(size)]
    swap_side = [(i, i ^ 2) for i in range(size)]
    along_z = [list(range(start, size, 4)) for start in range(4)]

    slot = jnp.concatenate(
        [prefix_keys.reshape(size, 1, PIECE, WIDTH), prefix_values.reshape(size, 1, PIECE, WIDTH)], axis=1
    )

    def halve(array, at, owner_at, swap):
        half = array.shape[0] // 2
        kept = lax.dynamic_slice_in_dim(array, at * half, half, 0)
        sent = lax.dynamic_slice_in_dim(array, (1 - at) * half, half, 0)
        got = lax.ppermute(sent, "rep", swap)
        return jnp.where(owner_at == at, kept, got)

    part = halve(slot, core, owner_core, swap_core)
    part = halve(part, side, owner_side, swap_side)
    part = lax.all_to_all(part, "rep", 0, 0, axis_index_groups=along_z, tiled=True)
    part = lax.dynamic_slice_in_dim(part, owner_z, 1, 0)
    own = lax.all_gather(part, "rep", axis_index_groups=along_z, tiled=True)

    from_side = lax.ppermute(own, "rep", swap_side)
    from_core = lax.ppermute(own, "rep", swap_core)
    from_both = lax.ppermute(from_side, "rep", swap_core)

    piece = own.shape[0] * PIECE
    shift_shape = jax.ShapeDtypeStruct((GROUP, rows, WIDTH), f32)
    total_shape = jax.ShapeDtypeStruct((GROUP, rows, 2 * WIDTH), f32)
    shift_spec = pl.BlockSpec((HEADS_STEP, rows, WIDTH), lambda i: (i, 0, 0))
    total_spec = pl.BlockSpec((HEADS_STEP, rows, 2 * WIDTH), lambda i: (i, 0, 0))
    suffix = (rotated_suffix_keys, suffix_values)
    shift, total = call(
        first_kernel, queries, (*suffix, own), (shift_shape, total_shape), (shift_spec, total_spec),
        [whole(suffix[0]), whole(suffix[1]), whole(own)], piece + rows,
    )
    for more in (from_core, from_side):
        total = call(
            next_kernel, queries, (shift, total, more), total_shape, total_spec,
            [shift_spec, total_spec, whole(more)], piece,
        )
    output = call(
        last_kernel, queries, (shift, total, from_both, *suffix, own, from_core, from_side),
        jax.ShapeDtypeStruct(queries.shape, bf16),
        pl.BlockSpec((rows, HEADS_STEP * WIDTH), lambda i: (0, i)),
        [shift_spec, total_spec, whole(from_both), whole(suffix[0]), whole(suffix[1]), whole(own), whole(own), whole(own)],
        piece,
    )
    return lax.all_to_all(output, "tp", split_axis=0, concat_axis=1, tiled=True)


def solution(mesh):
    in_specs = (P(), P("rep", "tp"), P("rep", "tp"), P("rep", "tp"), P("rep", "tp"), P("rep", "tp"))
    out_specs = P(("rep", "tp"), None)
    return jax.shard_map(local, mesh=mesh, in_specs=in_specs, out_specs=out_specs, check_vma=False)
```

```python
import functools
import math

import jax
import jax.numpy as jnp
from jax import lax
from jax.experimental import pallas as pl
from jax.experimental.pallas import tpu as pltpu
from jax.sharding import PartitionSpec as P

Q_HEADS = 64
KEY_VALUE_HEADS = 8
GROUP = Q_HEADS // KEY_VALUE_HEADS
WIDTH = 128
PIECE = 64
TILE = 1024
SCORE_SCALE = math.log2(math.e) / math.sqrt(WIDTH)
NEGATIVE = -1e30
LARGE = 1e30
NT = (((1,), (1,)), ((), ()))
f32, bf16 = jnp.float32, jnp.bfloat16


def with_ones(values):
    return jnp.concatenate([values, jnp.ones(values.shape, values.dtype)], axis=1)


def spread(column, count):
    return jnp.concatenate([column] * count, axis=1)


def flat(kv_ref, part):
    return kv_ref[:, part].reshape(kv_ref.shape[0] * kv_ref.shape[2], WIDTH)


def head_of(q_ref, head):
    return q_ref[:, head * WIDTH:(head + 1) * WIDTH]


def suffix_scores(query, keys):
    scores = lax.dot_general(query, keys, NT, preferred_element_type=f32) * SCORE_SCALE
    row = lax.broadcasted_iota(jnp.int32, scores.shape, 0)
    col = lax.broadcasted_iota(jnp.int32, scores.shape, 1)
    return jnp.where(col <= row, scores, NEGATIVE)


def add_piece(query, shift, kv_ref, total):
    keys, values = flat(kv_ref, 0), with_ones(flat(kv_ref, 1))
    wide = spread(shift, TILE // WIDTH)
    for start in range(0, keys.shape[0], TILE):
        scores = lax.dot_general(query, keys[start:start + TILE], NT, preferred_element_type=f32)
        weights = jnp.exp2(scores * SCORE_SCALE - wide).astype(bf16)
        total = total + jnp.dot(weights, values[start:start + TILE], preferred_element_type=f32)
    return total


def suffix_kernel(q_ref, k_ref, v_ref, shift_ref, total_ref):
    for head in range(GROUP):
        scores = suffix_scores(head_of(q_ref, head), k_ref[...])
        shift = jnp.broadcast_to(jnp.max(scores, axis=1, keepdims=True), (scores.shape[0], WIDTH))
        weights = jnp.exp2(scores - spread(shift, scores.shape[1] // WIDTH)).astype(bf16)
        shift_ref[head] = shift
        total_ref[head] = jnp.dot(weights, with_ones(v_ref[...]), preferred_element_type=f32)


def next_kernel(q_ref, shift_ref, total_in, kv_ref, total_ref):
    for head in range(GROUP):
        total_ref[head] = add_piece(head_of(q_ref, head), shift_ref[head], kv_ref, total_in[head])


def last_kernel(q_ref, shift_ref, total_in, kv_ref, k_ref, v_ref, other_ref, out_ref):
    worst = jnp.zeros(shift_ref.shape[1:], f32)
    for head in range(GROUP):
        total = add_piece(head_of(q_ref, head), shift_ref[head], kv_ref, total_in[head])
        weight = total[:, WIDTH:]
        worst = jnp.maximum(worst, jnp.where(weight < LARGE, 0.0, 1.0))
        out_ref[:, head * WIDTH:(head + 1) * WIDTH] = (total[:, :WIDTH] / weight).astype(bf16)

    @pl.when(jnp.max(worst) > 0.0)
    def _():
        def one_head(head, carry):
            at = pl.ds(pl.multiple_of(head * WIDTH, WIDTH), WIDTH)
            query = q_ref[:, at]

            def block(state, scores, values):
                shift, total = state
                newest = jnp.maximum(shift, jnp.max(scores, axis=1, keepdims=True))
                weights = jnp.exp2(scores - newest).astype(bf16)
                added = jnp.dot(weights, with_ones(values), preferred_element_type=f32)
                return newest, total * jnp.exp2(shift - newest) + added

            state = (jnp.full((query.shape[0], 1), NEGATIVE, f32), jnp.zeros((query.shape[0], 2 * WIDTH), f32))
            state = block(state, suffix_scores(query, k_ref[...]), v_ref[...])
            for ref in (other_ref, kv_ref):
                def step(i, state, ref=ref):
                    some = ref.at[pl.ds(i * 8, 8)]
                    scores = lax.dot_general(query, flat(some, 0), NT, preferred_element_type=f32) * SCORE_SCALE
                    return block(state, scores, flat(some, 1))

                state = lax.fori_loop(0, ref.shape[0] // 8, step, state)
            total = state[1]
            out_ref[:, at] = (total[:, :WIDTH] / total[:, WIDTH:]).astype(bf16)
            return carry

        lax.fori_loop(0, GROUP, one_head, 0)


def call(kernel, out_shape, keys, *args):
    flops = 8 * args[0].shape[0] * GROUP * keys * WIDTH
    in_vmem = pl.BlockSpec(memory_space=pltpu.VMEM)
    return pl.pallas_call(
        kernel,
        in_specs=[in_vmem] * len(args),
        out_specs=jax.tree.map(lambda _: in_vmem, out_shape),
        out_shape=out_shape,
        compiler_params=pltpu.CompilerParams(vmem_limit_bytes=24 * 1024 * 1024),
        cost_estimate=pl.CostEstimate(flops=flops, bytes_accessed=4 * 1024 * 1024, transcendentals=0),
    )(*args)


def local(owner, queries, rotated_suffix_keys, suffix_values, prefix_keys, prefix_values):
    rep, tp = lax.axis_index("rep"), lax.axis_index("tp")
    size = lax.axis_size("rep")
    rows = queries.shape[0]
    mine = owner[tp]
    owner_core, owner_side, owner_z = mine % 2, (mine // 2) % 2, mine // 4

    def place(z, side, core):
        return 4 * z + 2 * side + core

    near = [[place(2 * a + b, s, c) for b in range(2) for s in range(2)] for a in range(8) for c in range(2)]
    far = [[place(2 * a + b, s, c) for a in range(8)] for b in range(2) for s in range(2) for c in range(2)]
    swap_core = [(i, i ^ 1) for i in range(size)]

    def exchange(array, groups):
        return lax.all_to_all(array, "rep", 0, 0, axis_index_groups=groups, tiled=True)

    def pick(array, at, count):
        share = array.shape[0] // count
        return lax.dynamic_slice_in_dim(array, at * share, share, 0)

    def copies(array, count):
        many = jnp.broadcast_to(array[None], (count, *array.shape))
        return many.reshape(count * array.shape[0], *array.shape[1:])

    shape = (prefix_keys.shape[0] // PIECE, 1, PIECE, WIDTH)
    slot = jnp.concatenate([prefix_keys.reshape(shape), prefix_values.reshape(shape)], axis=1)
    half = shape[0] // 2
    core = rep % 2
    kept = lax.dynamic_slice_in_dim(slot, core * half, half, 0)
    sent = lax.dynamic_slice_in_dim(slot, (1 - core) * half, half, 0)
    part = jnp.where(owner_core == core, kept, lax.ppermute(sent, "rep", swap_core))
    part = pick(exchange(part, near), (owner_z % 2) * 2 + owner_side, 4)
    part = pick(exchange(part, far), owner_z // 2, 8)
    part = exchange(copies(part, 8), far)
    first = exchange(copies(part, 4), near)
    second = lax.ppermute(first, "rep", swap_core)

    shift_shape = jax.ShapeDtypeStruct((GROUP, rows, WIDTH), f32)
    total_shape = jax.ShapeDtypeStruct((GROUP, rows, 2 * WIDTH), f32)
    suffix = (rotated_suffix_keys, suffix_values)
    shift, total = call(suffix_kernel, (shift_shape, total_shape), rows, queries, *suffix)
    total = call(next_kernel, total_shape, half * PIECE, queries, shift, total, first)
    output = call(
        last_kernel, jax.ShapeDtypeStruct(queries.shape, bf16), half * PIECE,
        queries, shift, total, second, *suffix, first,
    )
    return lax.all_to_all(output, "tp", split_axis=0, concat_axis=1, tiled=True)


def solution(mesh):
    in_specs = (P(), P("rep", "tp"), P("rep", "tp"), P("rep", "tp"), P("rep", "tp"), P("rep", "tp"))
    out_specs = P(("rep", "tp"), None)
    return jax.shard_map(local, mesh=mesh, in_specs=in_specs, out_specs=out_specs, check_vma=False)
```

```python
import functools
import math

import jax
import jax.numpy as jnp
from jax import lax
from jax.experimental import pallas as pl
from jax.experimental.pallas import tpu as pltpu
from jax.sharding import PartitionSpec as P

Q_HEADS = 64
KEY_VALUE_HEADS = 8
GROUP = Q_HEADS // KEY_VALUE_HEADS
WIDTH = 128
PIECE = 64
TILE = 1024
SCORE_SCALE = math.log2(math.e) / math.sqrt(WIDTH)
NEGATIVE = -1e30
LARGE = 1e30
NT = (((1,), (1,)), ((), ()))
f32, bf16 = jnp.float32, jnp.bfloat16


def with_ones(values):
    return jnp.concatenate([values, jnp.ones(values.shape, values.dtype)], axis=1)


def spread(column, count):
    return jnp.concatenate([column] * count, axis=1)


def flat(kv_ref, part):
    return kv_ref[:, part].reshape(kv_ref.shape[0] * kv_ref.shape[2], WIDTH)


def head_of(q_ref, head):
    return q_ref[:, head * WIDTH:(head + 1) * WIDTH]


def suffix_scores(query, keys):
    scores = lax.dot_general(query, keys, NT, preferred_element_type=f32) * SCORE_SCALE
    row = lax.broadcasted_iota(jnp.int32, scores.shape, 0)
    col = lax.broadcasted_iota(jnp.int32, scores.shape, 1)
    return jnp.where(col <= row, scores, NEGATIVE)


def add_piece(query, shift, kv_ref, total):
    keys, values = flat(kv_ref, 0), with_ones(flat(kv_ref, 1))
    wide = spread(shift, TILE // WIDTH)
    for start in range(0, keys.shape[0], TILE):
        scores = lax.dot_general(query, keys[start:start + TILE], NT, preferred_element_type=f32)
        weights = jnp.exp2(scores * SCORE_SCALE - wide).astype(bf16)
        total = total + jnp.dot(weights, values[start:start + TILE], preferred_element_type=f32)
    return total


def suffix_kernel(q_ref, k_ref, v_ref, shift_ref, total_ref):
    for head in range(GROUP):
        scores = suffix_scores(head_of(q_ref, head), k_ref[...])
        shift = jnp.broadcast_to(jnp.max(scores, axis=1, keepdims=True), (scores.shape[0], WIDTH))
        weights = jnp.exp2(scores - spread(shift, scores.shape[1] // WIDTH)).astype(bf16)
        shift_ref[head] = shift
        total_ref[head] = jnp.dot(weights, with_ones(v_ref[...]), preferred_element_type=f32)


def next_kernel(q_ref, shift_ref, total_in, kv_ref, total_ref):
    for head in range(GROUP):
        total_ref[head] = add_piece(head_of(q_ref, head), shift_ref[head], kv_ref, total_in[head])


def last_kernel(q_ref, shift_ref, total_in, kv_ref, k_ref, v_ref, other_ref, out_ref):
    worst = jnp.zeros(shift_ref.shape[1:], f32)
    for head in range(GROUP):
        total = add_piece(head_of(q_ref, head), shift_ref[head], kv_ref, total_in[head])
        weight = total[:, WIDTH:]
        worst = jnp.maximum(worst, jnp.where(weight < LARGE, 0.0, 1.0))
        out_ref[:, head * WIDTH:(head + 1) * WIDTH] = (total[:, :WIDTH] / weight).astype(bf16)

    @pl.when(jnp.max(worst) > 0.0)
    def _():
        def one_head(head, carry):
            at = pl.ds(pl.multiple_of(head * WIDTH, WIDTH), WIDTH)
            query = q_ref[:, at]

            def block(state, scores, values):
                shift, total = state
                newest = jnp.maximum(shift, jnp.max(scores, axis=1, keepdims=True))
                weights = jnp.exp2(scores - newest).astype(bf16)
                added = jnp.dot(weights, with_ones(values), preferred_element_type=f32)
                return newest, total * jnp.exp2(shift - newest) + added

            state = (jnp.full((query.shape[0], 1), NEGATIVE, f32), jnp.zeros((query.shape[0], 2 * WIDTH), f32))
            state = block(state, suffix_scores(query, k_ref[...]), v_ref[...])
            for ref in (other_ref, kv_ref):
                def step(i, state, ref=ref):
                    some = ref.at[pl.ds(i * 8, 8)]
                    scores = lax.dot_general(query, flat(some, 0), NT, preferred_element_type=f32) * SCORE_SCALE
                    return block(state, scores, flat(some, 1))

                state = lax.fori_loop(0, ref.shape[0] // 8, step, state)
            total = state[1]
            out_ref[:, at] = (total[:, :WIDTH] / total[:, WIDTH:]).astype(bf16)
            return carry

        lax.fori_loop(0, GROUP, one_head, 0)


def call(kernel, out_shape, keys, *args):
    flops = 8 * args[0].shape[0] * GROUP * keys * WIDTH
    in_vmem = pl.BlockSpec(memory_space=pltpu.VMEM)
    return pl.pallas_call(
        kernel,
        in_specs=[in_vmem] * len(args),
        out_specs=jax.tree.map(lambda _: in_vmem, out_shape),
        out_shape=out_shape,
        compiler_params=pltpu.CompilerParams(vmem_limit_bytes=24 * 1024 * 1024),
        cost_estimate=pl.CostEstimate(flops=flops, bytes_accessed=4 * 1024 * 1024, transcendentals=0),
    )(*args)


def local(owner, queries, rotated_suffix_keys, suffix_values, prefix_keys, prefix_values):
    rep, tp = lax.axis_index("rep"), lax.axis_index("tp")
    size = lax.axis_size("rep")
    rows = queries.shape[0]
    mine = owner[tp]

    def place(z, side, core):
        return 4 * z + 2 * side + core

    near = [[place(2 * a + b, s, c) for b in range(2) for s in range(2)] for a in range(8) for c in range(2)]
    far = [[place(2 * a + b, s, c) for a in range(8)] for b in range(2) for s in range(2) for c in range(2)]
    swap_core = [(i, i ^ 1) for i in range(size)]

    def exchange(array, groups):
        return lax.all_to_all(array, "rep", 0, 0, axis_index_groups=groups, tiled=True)

    def pick(array, at, count):
        share = array.shape[0] // count
        return lax.dynamic_slice_in_dim(array, at * share, share, 0, allow_negative_indices=False)

    def copies(array, count):
        many = jnp.broadcast_to(array[None], (count, *array.shape))
        return many.reshape(count * array.shape[0], *array.shape[1:])

    count = prefix_keys.shape[0] // 2
    half = count // PIECE
    core = rep & 1
    shape = (half, 2, PIECE, WIDTH)
    is_key = lax.broadcasted_iota(jnp.int32, shape, 1) == 0

    def half_of(which):
        at = which * count
        keys, values = (
            lax.dynamic_slice_in_dim(array, at, count, 0, allow_negative_indices=False).reshape(half, 1, PIECE, WIDTH)
            for array in (prefix_keys, prefix_values)
        )
        return jnp.where(is_key, keys, values)

    in_near = (mine >> 1) & 3
    in_far = mine >> 3
    owner_core = mine - 8 * in_far - 2 * in_near
    got = lax.ppermute(half_of(1 - core), "rep", swap_core)
    part = jnp.where(owner_core == core, half_of(core), got)
    part = pick(exchange(part, near), in_near, 4)
    part = jnp.where(in_far == rep >> 3, part, jnp.zeros_like(part)).astype(f32)
    part = lax.psum(part, "rep", axis_index_groups=far).astype(bf16)
    first = exchange(copies(part, 4), near)
    second = lax.ppermute(first, "rep", swap_core)

    shift_shape = jax.ShapeDtypeStruct((GROUP, rows, WIDTH), f32)
    total_shape = jax.ShapeDtypeStruct((GROUP, rows, 2 * WIDTH), f32)
    suffix = (rotated_suffix_keys, suffix_values)
    shift, total = call(suffix_kernel, (shift_shape, total_shape), rows, queries, *suffix)
    total = call(next_kernel, total_shape, half * PIECE, queries, shift, total, first)
    output = call(
        last_kernel, jax.ShapeDtypeStruct(queries.shape, bf16), half * PIECE,
        queries, shift, total, second, *suffix, first,
    )
    return lax.all_to_all(output, "tp", split_axis=0, concat_axis=1, tiled=True)


def solution(mesh):
    in_specs = (P(), P("rep", "tp"), P("rep", "tp"), P("rep", "tp"), P("rep", "tp"), P("rep", "tp"))
    out_specs = P(("rep", "tp"), None)
    return jax.shard_map(local, mesh=mesh, in_specs=in_specs, out_specs=out_specs, check_vma=False)
```

```python
import functools
import math

import jax
import jax.numpy as jnp
from jax import lax
from jax.experimental import pallas as pl
from jax.experimental.pallas import tpu as pltpu
from jax.sharding import PartitionSpec as P

Q_HEADS = 64
KEY_VALUE_HEADS = 8
GROUP = Q_HEADS // KEY_VALUE_HEADS
WIDTH = 128
PIECE = 64
TILE = 1024
SCORE_SCALE = math.log2(math.e) / math.sqrt(WIDTH)
NEGATIVE = -1e30
LARGE = 1e30
NT = (((1,), (1,)), ((), ()))
f32, bf16 = jnp.float32, jnp.bfloat16


def with_ones(values):
    return jnp.concatenate([values, jnp.ones(values.shape, values.dtype)], axis=1)


def spread(column, count):
    return jnp.concatenate([column] * count, axis=1)


def flat(kv_ref, part):
    return kv_ref[:, part].reshape(kv_ref.shape[0] * kv_ref.shape[2], WIDTH)


def head_of(q_ref, head):
    return q_ref[:, head * WIDTH:(head + 1) * WIDTH]


def suffix_scores(query, keys):
    scores = lax.dot_general(query, keys, NT, preferred_element_type=f32) * SCORE_SCALE
    row = lax.broadcasted_iota(jnp.int32, scores.shape, 0)
    col = lax.broadcasted_iota(jnp.int32, scores.shape, 1)
    return jnp.where(col <= row, scores, NEGATIVE)


def add_piece(query, shift, kv_ref, total):
    keys, values = flat(kv_ref, 0), with_ones(flat(kv_ref, 1))
    wide = spread(shift, TILE // WIDTH)
    for start in range(0, keys.shape[0], TILE):
        scores = lax.dot_general(query, keys[start:start + TILE], NT, preferred_element_type=f32)
        weights = jnp.exp2(scores * SCORE_SCALE - wide).astype(bf16)
        total = total + jnp.dot(weights, values[start:start + TILE], preferred_element_type=f32)
    return total


def first_kernel(q_ref, k_ref, v_ref, kv_ref, shift_ref, total_ref):
    for head in range(GROUP):
        query = head_of(q_ref, head)
        scores = suffix_scores(query, k_ref[...])
        shift = jnp.broadcast_to(jnp.max(scores, axis=1, keepdims=True), (scores.shape[0], WIDTH))
        weights = jnp.exp2(scores - spread(shift, scores.shape[1] // WIDTH)).astype(bf16)
        total = jnp.dot(weights, with_ones(v_ref[...]), preferred_element_type=f32)
        shift_ref[head] = shift
        total_ref[head] = add_piece(query, shift, kv_ref, total)


def last_kernel(q_ref, shift_ref, total_in, kv_ref, k_ref, v_ref, other_ref, out_ref):
    worst = jnp.zeros(shift_ref.shape[1:], f32)
    for head in range(GROUP):
        total = add_piece(head_of(q_ref, head), shift_ref[head], kv_ref, total_in[head])
        weight = total[:, WIDTH:]
        worst = jnp.maximum(worst, jnp.where(weight < LARGE, 0.0, 1.0))
        out_ref[:, head * WIDTH:(head + 1) * WIDTH] = (total[:, :WIDTH] / weight).astype(bf16)

    @pl.when(jnp.max(worst) > 0.0)
    def _():
        def one_head(head, carry):
            at = pl.ds(pl.multiple_of(head * WIDTH, WIDTH), WIDTH)
            query = q_ref[:, at]

            def block(state, scores, values):
                shift, total = state
                newest = jnp.maximum(shift, jnp.max(scores, axis=1, keepdims=True))
                weights = jnp.exp2(scores - newest).astype(bf16)
                added = jnp.dot(weights, with_ones(values), preferred_element_type=f32)
                return newest, total * jnp.exp2(shift - newest) + added

            state = (jnp.full((query.shape[0], 1), NEGATIVE, f32), jnp.zeros((query.shape[0], 2 * WIDTH), f32))
            state = block(state, suffix_scores(query, k_ref[...]), v_ref[...])
            for ref in (other_ref, kv_ref):
                def step(i, state, ref=ref):
                    some = ref.at[pl.ds(i * 8, 8)]
                    scores = lax.dot_general(query, flat(some, 0), NT, preferred_element_type=f32) * SCORE_SCALE
                    return block(state, scores, flat(some, 1))

                state = lax.fori_loop(0, ref.shape[0] // 8, step, state)
            total = state[1]
            out_ref[:, at] = (total[:, :WIDTH] / total[:, WIDTH:]).astype(bf16)
            return carry

        lax.fori_loop(0, GROUP, one_head, 0)


def call(kernel, out_shape, keys, *args):
    flops = 8 * args[0].shape[0] * GROUP * keys * WIDTH
    in_vmem = pl.BlockSpec(memory_space=pltpu.VMEM)
    return pl.pallas_call(
        kernel,
        in_specs=[in_vmem] * len(args),
        out_specs=jax.tree.map(lambda _: in_vmem, out_shape),
        out_shape=out_shape,
        compiler_params=pltpu.CompilerParams(vmem_limit_bytes=24 * 1024 * 1024),
        cost_estimate=pl.CostEstimate(flops=flops, bytes_accessed=4 * 1024 * 1024, transcendentals=0),
    )(*args)


def local(owner, queries, rotated_suffix_keys, suffix_values, prefix_keys, prefix_values):
    rep, tp = lax.axis_index("rep"), lax.axis_index("tp")
    size = lax.axis_size("rep")
    rows = queries.shape[0]
    mine = owner[tp]

    def place(z, side, core):
        return 4 * z + 2 * side + core

    near = [[place(2 * a + b, s, c) for b in range(2) for s in range(2)] for a in range(8) for c in range(2)]
    far = [[place(2 * a + b, s, c) for a in range(8)] for b in range(2) for s in range(2) for c in range(2)]
    swap_core = [(i, i ^ 1) for i in range(size)]

    def exchange(array, groups):
        return lax.all_to_all(array, "rep", 0, 0, axis_index_groups=groups, tiled=True)

    def copies(array, count):
        many = jnp.broadcast_to(array[None], (count, *array.shape))
        return many.reshape(count * array.shape[0], *array.shape[1:])

    count = prefix_keys.shape[0] // 2
    half = count // PIECE
    core = rep & 1
    shape = (half, 2, PIECE, WIDTH)
    is_key = lax.broadcasted_iota(jnp.int32, shape, 1) == 0

    def half_of(which):
        at = which * count
        keys, values = (
            lax.dynamic_slice_in_dim(array, at, count, 0, allow_negative_indices=False).reshape(half, 1, PIECE, WIDTH)
            for array in (prefix_keys, prefix_values)
        )
        return jnp.where(is_key, keys, values)

    in_far = mine >> 3
    share = half // 4
    in_near = ((mine >> 1) & 3) * share
    owner_core = mine - 8 * in_far - 2 * (in_near // share)
    here = in_far == rep >> 3
    got = lax.ppermute(half_of(1 - core), "rep", swap_core)
    part = jnp.where(here & (owner_core == core), half_of(owner_core), got)
    part = lax.dynamic_slice_in_dim(exchange(part, near), in_near, share, 0, allow_negative_indices=False)
    part = jnp.where(here, part, jnp.zeros_like(part)).astype(f32)
    part = lax.psum(part, "rep", axis_index_groups=far).astype(bf16)
    first = exchange(copies(part, 4), near)
    second = lax.ppermute(first, "rep", swap_core)

    shift_shape = jax.ShapeDtypeStruct((GROUP, rows, WIDTH), f32)
    total_shape = jax.ShapeDtypeStruct((GROUP, rows, 2 * WIDTH), f32)
    suffix = (rotated_suffix_keys, suffix_values)
    shift, total = call(first_kernel, (shift_shape, total_shape), rows + half * PIECE, queries, *suffix, first)
    output = call(
        last_kernel, jax.ShapeDtypeStruct(queries.shape, bf16), half * PIECE,
        queries, shift, total, second, *suffix, first,
    )
    return lax.all_to_all(output, "tp", split_axis=0, concat_axis=1, tiled=True)


def solution(mesh):
    in_specs = (P(), P("rep", "tp"), P("rep", "tp"), P("rep", "tp"), P("rep", "tp"), P("rep", "tp"))
    out_specs = P(("rep", "tp"), None)
    return jax.shard_map(local, mesh=mesh, in_specs=in_specs, out_specs=out_specs, check_vma=False)
```

```python
import functools
import math

import jax
import jax.numpy as jnp
from jax import lax
from jax.experimental import pallas as pl
from jax.experimental.pallas import tpu as pltpu
from jax.sharding import PartitionSpec as P

Q_HEADS = 64
KEY_VALUE_HEADS = 8
GROUP = Q_HEADS // KEY_VALUE_HEADS
WIDTH = 128
PIECE = 64
TILE = 1024
SCORE_SCALE = math.log2(math.e) / math.sqrt(WIDTH)
NEGATIVE = -1e30
LARGE = 1e30
NT = (((1,), (1,)), ((), ()))
f32, bf16 = jnp.float32, jnp.bfloat16


def with_ones(values):
    return jnp.concatenate([values, jnp.ones(values.shape, values.dtype)], axis=1)


def spread(column, count):
    return jnp.concatenate([column] * count, axis=1)


def flat(kv_ref, part):
    return kv_ref[:, part].reshape(kv_ref.shape[0] * kv_ref.shape[2], WIDTH)


def head_of(q_ref, head):
    return q_ref[:, head * WIDTH:(head + 1) * WIDTH]


def suffix_scores(query, keys):
    scores = lax.dot_general(query, keys, NT, preferred_element_type=f32) * SCORE_SCALE
    row = lax.broadcasted_iota(jnp.int32, scores.shape, 0)
    col = lax.broadcasted_iota(jnp.int32, scores.shape, 1)
    return jnp.where(col <= row, scores, NEGATIVE)


def add_piece(query, shift, kv_ref, total):
    keys, values = flat(kv_ref, 0), with_ones(flat(kv_ref, 1))
    wide = spread(shift, TILE // WIDTH)
    for start in range(0, keys.shape[0], TILE):
        scores = lax.dot_general(query, keys[start:start + TILE], NT, preferred_element_type=f32)
        weights = jnp.exp2(scores * SCORE_SCALE - wide).astype(bf16)
        total = total + jnp.dot(weights, values[start:start + TILE], preferred_element_type=f32)
    return total


def first_kernel(q_ref, k_ref, v_ref, kv_ref, shift_ref, total_ref):
    for head in range(GROUP):
        query = head_of(q_ref, head)
        scores = suffix_scores(query, k_ref[...])
        shift = jnp.broadcast_to(jnp.max(scores, axis=1, keepdims=True), (scores.shape[0], WIDTH))
        weights = jnp.exp2(scores - spread(shift, scores.shape[1] // WIDTH)).astype(bf16)
        total = jnp.dot(weights, with_ones(v_ref[...]), preferred_element_type=f32)
        shift_ref[head] = shift
        total_ref[head] = add_piece(query, shift, kv_ref, total)


def last_kernel(q_ref, shift_ref, total_in, kv_ref, k_ref, v_ref, other_ref, out_ref):
    worst = jnp.zeros(shift_ref.shape[1:], f32)
    for head in range(GROUP):
        total = add_piece(head_of(q_ref, head), shift_ref[head], kv_ref, total_in[head])
        weight = total[:, WIDTH:]
        worst = jnp.maximum(worst, jnp.where(weight < LARGE, 0.0, 1.0))
        out_ref[:, head * WIDTH:(head + 1) * WIDTH] = (total[:, :WIDTH] / weight).astype(bf16)

    @pl.when(jnp.max(worst) > 0.0)
    def _():
        def one_head(head, carry):
            at = pl.ds(pl.multiple_of(head * WIDTH, WIDTH), WIDTH)
            query = q_ref[:, at]

            def block(state, scores, values):
                shift, total = state
                newest = jnp.maximum(shift, jnp.max(scores, axis=1, keepdims=True))
                weights = jnp.exp2(scores - newest).astype(bf16)
                added = jnp.dot(weights, with_ones(values), preferred_element_type=f32)
                return newest, total * jnp.exp2(shift - newest) + added

            state = (jnp.full((query.shape[0], 1), NEGATIVE, f32), jnp.zeros((query.shape[0], 2 * WIDTH), f32))
            state = block(state, suffix_scores(query, k_ref[...]), v_ref[...])
            for ref in (other_ref, kv_ref):
                def step(i, state, ref=ref):
                    some = ref.at[pl.ds(i * 8, 8)]
                    scores = lax.dot_general(query, flat(some, 0), NT, preferred_element_type=f32) * SCORE_SCALE
                    return block(state, scores, flat(some, 1))

                state = lax.fori_loop(0, ref.shape[0] // 8, step, state)
            total = state[1]
            out_ref[:, at] = (total[:, :WIDTH] / total[:, WIDTH:]).astype(bf16)
            return carry

        lax.fori_loop(0, GROUP, one_head, 0)


def call(kernel, out_shape, keys, *args):
    flops = 8 * args[0].shape[0] * GROUP * keys * WIDTH
    in_vmem = pl.BlockSpec(memory_space=pltpu.VMEM)
    return pl.pallas_call(
        kernel,
        in_specs=[in_vmem] * len(args),
        out_specs=jax.tree.map(lambda _: in_vmem, out_shape),
        out_shape=out_shape,
        compiler_params=pltpu.CompilerParams(vmem_limit_bytes=24 * 1024 * 1024),
        cost_estimate=pl.CostEstimate(flops=flops, bytes_accessed=4 * 1024 * 1024, transcendentals=0),
    )(*args)


def local(owner, queries, rotated_suffix_keys, suffix_values, prefix_keys, prefix_values):
    rep, tp = lax.axis_index("rep"), lax.axis_index("tp")
    size = lax.axis_size("rep")
    rows = queries.shape[0]
    mine = owner[tp]

    def place(z, side, core):
        return 4 * z + 2 * side + core

    near = [[place(2 * a + b, s, c) for b in range(2) for s in range(2)] for a in range(8) for c in range(2)]
    far = [[place(2 * a + b, s, c) for a in range(8)] for b in range(2) for s in range(2) for c in range(2)]
    swap_core = [(i, i ^ 1) for i in range(size)]

    def exchange(array, groups):
        return lax.all_to_all(array, "rep", 0, 0, axis_index_groups=groups, tiled=True)

    def copies(array, count):
        many = jnp.broadcast_to(array[None], (count, *array.shape))
        return many.reshape(count * array.shape[0], *array.shape[1:])

    count = prefix_keys.shape[0] // 2
    half = count // PIECE
    core = rep & 1
    shape = (half, 2, PIECE, WIDTH)
    is_key = lax.broadcasted_iota(jnp.int32, shape, 1) == 0

    def half_of(which):
        at = which * count
        keys, values = (
            lax.dynamic_slice_in_dim(array, at, count, 0, allow_negative_indices=False).reshape(half, 1, PIECE, WIDTH)
            for array in (prefix_keys, prefix_values)
        )
        return jnp.where(is_key, keys, values)

    in_far = mine >> 3
    share = half // 4
    in_near = ((mine >> 1) & 3) * share
    owner_core = mine - 8 * in_far - 2 * (in_near // share)
    here = in_far == rep >> 3
    got = lax.ppermute(half_of(1 - core), "rep", swap_core)
    part = jnp.where(here & (owner_core == core), half_of(core), got)
    part = lax.dynamic_slice_in_dim(exchange(part, near), in_near, share, 0, allow_negative_indices=False)
    part = jnp.where(here, part, jnp.zeros_like(part)).astype(f32)
    part = lax.psum(part, "rep", axis_index_groups=far).astype(bf16)
    first = exchange(copies(part, 4), near)
    second = lax.ppermute(first, "rep", swap_core)

    shift_shape = jax.ShapeDtypeStruct((GROUP, rows, WIDTH), f32)
    total_shape = jax.ShapeDtypeStruct((GROUP, rows, 2 * WIDTH), f32)
    suffix = (rotated_suffix_keys, suffix_values)
    shift, total = call(first_kernel, (shift_shape, total_shape), rows + half * PIECE, queries, *suffix, first)
    output = call(
        last_kernel, jax.ShapeDtypeStruct(queries.shape, bf16), half * PIECE,
        queries, shift, total, second, *suffix, first,
    )
    return lax.all_to_all(output, "tp", split_axis=0, concat_axis=1, tiled=True)


def solution(mesh):
    in_specs = (P(), P("rep", "tp"), P("rep", "tp"), P("rep", "tp"), P("rep", "tp"), P("rep", "tp"))
    out_specs = P(("rep", "tp"), None)
    return jax.shard_map(local, mesh=mesh, in_specs=in_specs, out_specs=out_specs, check_vma=False)
```

```python
import functools
import math

import jax
import jax.numpy as jnp
from jax import lax
from jax.experimental import pallas as pl
from jax.experimental.pallas import tpu as pltpu
from jax.sharding import PartitionSpec as P

Q_HEADS = 64
KEY_VALUE_HEADS = 8
GROUP = Q_HEADS // KEY_VALUE_HEADS
WIDTH = 128
PIECE = 64
TILE = 1024
SCORE_SCALE = math.log2(math.e) / math.sqrt(WIDTH)
NEGATIVE = -1e30
LARGE = 1e30
NT = (((1,), (1,)), ((), ()))
f32, bf16 = jnp.float32, jnp.bfloat16


def with_ones(values):
    return jnp.concatenate([values, jnp.ones(values.shape, values.dtype)], axis=1)


def spread(column, count):
    return jnp.concatenate([column] * count, axis=1)


def flat(kv_ref, part):
    return kv_ref[:, part].reshape(kv_ref.shape[0] * kv_ref.shape[2], WIDTH)


def head_of(q_ref, head):
    return q_ref[:, head * WIDTH:(head + 1) * WIDTH]


def suffix_scores(query, keys):
    scores = lax.dot_general(query, keys, NT, preferred_element_type=f32) * SCORE_SCALE
    row = lax.broadcasted_iota(jnp.int32, scores.shape, 0)
    col = lax.broadcasted_iota(jnp.int32, scores.shape, 1)
    return jnp.where(col <= row, scores, NEGATIVE)


def add_piece(query, shift, kv_ref, total):
    keys, values = flat(kv_ref, 0), with_ones(flat(kv_ref, 1))
    wide = spread(shift, TILE // WIDTH)
    for start in range(0, keys.shape[0], TILE):
        scores = lax.dot_general(query, keys[start:start + TILE], NT, preferred_element_type=f32)
        weights = jnp.exp2(scores * SCORE_SCALE - wide).astype(bf16)
        total = total + jnp.dot(weights, values[start:start + TILE], preferred_element_type=f32)
    return total


def first_kernel(q_ref, k_ref, v_ref, kv_ref, shift_ref, total_ref):
    for head in range(GROUP):
        query = head_of(q_ref, head)
        scores = suffix_scores(query, k_ref[...])
        shift = jnp.broadcast_to(jnp.max(scores, axis=1, keepdims=True), (scores.shape[0], WIDTH))
        weights = jnp.exp2(scores - spread(shift, scores.shape[1] // WIDTH)).astype(bf16)
        total = jnp.dot(weights, with_ones(v_ref[...]), preferred_element_type=f32)
        shift_ref[head] = shift
        total_ref[head] = add_piece(query, shift, kv_ref, total)


def last_kernel(q_ref, shift_ref, total_in, kv_ref, k_ref, v_ref, other_ref, out_ref):
    worst = jnp.zeros(shift_ref.shape[1:], f32)
    for head in range(GROUP):
        total = add_piece(head_of(q_ref, head), shift_ref[head], kv_ref, total_in[head])
        weight = total[:, WIDTH:]
        worst = jnp.maximum(worst, jnp.where(weight < LARGE, 0.0, 1.0))
        out_ref[:, head * WIDTH:(head + 1) * WIDTH] = (total[:, :WIDTH] / weight).astype(bf16)

    @pl.when(jnp.max(worst) > 0.0)
    def _():
        def one_head(head, carry):
            at = pl.ds(pl.multiple_of(head * WIDTH, WIDTH), WIDTH)
            query = q_ref[:, at]

            def block(state, scores, values):
                shift, total = state
                newest = jnp.maximum(shift, jnp.max(scores, axis=1, keepdims=True))
                weights = jnp.exp2(scores - newest).astype(bf16)
                added = jnp.dot(weights, with_ones(values), preferred_element_type=f32)
                return newest, total * jnp.exp2(shift - newest) + added

            state = (jnp.full((query.shape[0], 1), NEGATIVE, f32), jnp.zeros((query.shape[0], 2 * WIDTH), f32))
            state = block(state, suffix_scores(query, k_ref[...]), v_ref[...])
            for ref in (other_ref, kv_ref):
                def step(i, state, ref=ref):
                    some = ref.at[pl.ds(i * 8, 8)]
                    scores = lax.dot_general(query, flat(some, 0), NT, preferred_element_type=f32) * SCORE_SCALE
                    return block(state, scores, flat(some, 1))

                state = lax.fori_loop(0, ref.shape[0] // 8, step, state)
            total = state[1]
            out_ref[:, at] = (total[:, :WIDTH] / total[:, WIDTH:]).astype(bf16)
            return carry

        lax.fori_loop(0, GROUP, one_head, 0)


def call(kernel, out_shape, keys, *args):
    flops = 8 * args[0].shape[0] * GROUP * keys * WIDTH
    in_vmem = pl.BlockSpec(memory_space=pltpu.VMEM)
    return pl.pallas_call(
        kernel,
        in_specs=[in_vmem] * len(args),
        out_specs=jax.tree.map(lambda _: in_vmem, out_shape),
        out_shape=out_shape,
        compiler_params=pltpu.CompilerParams(vmem_limit_bytes=24 * 1024 * 1024),
        cost_estimate=pl.CostEstimate(flops=flops, bytes_accessed=4 * 1024 * 1024, transcendentals=0),
    )(*args)


def local(owner, queries, rotated_suffix_keys, suffix_values, prefix_keys, prefix_values):
    rep, tp = lax.axis_index("rep"), lax.axis_index("tp")
    size = lax.axis_size("rep")
    rows = queries.shape[0]
    mine = owner[tp]

    def place(z, side, core):
        return 4 * z + 2 * side + core

    near = [[place(2 * a + b, s, c) for b in range(2) for s in range(2)] for a in range(8) for c in range(2)]
    far = [[place(2 * a + b, s, c) for a in range(8)] for b in range(2) for s in range(2) for c in range(2)]
    swap_core = [(i, i ^ 1) for i in range(size)]

    def exchange(array, groups):
        return lax.all_to_all(array, "rep", 0, 0, axis_index_groups=groups, tiled=True)

    def copies(array, count):
        many = jnp.broadcast_to(array[None], (count, *array.shape))
        return many.reshape(count * array.shape[0], *array.shape[1:])

    count = prefix_keys.shape[0] // 2
    half = count // PIECE
    core = rep & 1
    shape = (half, 2, PIECE, WIDTH)
    is_key = lax.broadcasted_iota(jnp.int32, shape, 1) == 0

    def half_of(which):
        at = which * count
        keys, values = (
            lax.dynamic_slice_in_dim(array, at, count, 0, allow_negative_indices=False).reshape(half, 1, PIECE, WIDTH)
            for array in (prefix_keys, prefix_values)
        )
        return jnp.where(is_key, keys, values)

    in_far = mine >> 3
    share = half // 4
    in_near = ((mine >> 1) & 3) * share
    owner_core = mine - 8 * in_far - 2 * (in_near // share)
    here = in_far == rep >> 3

    got = lax.ppermute(half_of(1 - core), "rep", swap_core)
    kept = half_of(core)

    def scatter():
        part = jnp.where(owner_core == core, kept, got)
        part = exchange(part, near)
        return lax.dynamic_slice_in_dim(part, in_near, share, 0, allow_negative_indices=False).astype(f32)

    def nothing():
        return jnp.zeros((share, 2, PIECE, WIDTH), f32)

    part = lax.cond(here, scatter, nothing)
    part = lax.psum(part, "rep", axis_index_groups=far).astype(bf16)
    first = exchange(copies(part, 4), near)
    second = lax.ppermute(first, "rep", swap_core)

    shift_shape = jax.ShapeDtypeStruct((GROUP, rows, WIDTH), f32)
    total_shape = jax.ShapeDtypeStruct((GROUP, rows, 2 * WIDTH), f32)
    suffix = (rotated_suffix_keys, suffix_values)
    shift, total = call(first_kernel, (shift_shape, total_shape), rows + half * PIECE, queries, *suffix, first)
    output = call(
        last_kernel, jax.ShapeDtypeStruct(queries.shape, bf16), half * PIECE,
        queries, shift, total, second, *suffix, first,
    )
    return lax.all_to_all(output, "tp", split_axis=0, concat_axis=1, tiled=True)


def solution(mesh):
    in_specs = (P(), P("rep", "tp"), P("rep", "tp"), P("rep", "tp"), P("rep", "tp"), P("rep", "tp"))
    out_specs = P(("rep", "tp"), None)
    return jax.shard_map(local, mesh=mesh, in_specs=in_specs, out_specs=out_specs, check_vma=False)
```

```python
import functools
import math

import jax
import jax.numpy as jnp
from jax import lax
from jax.experimental import pallas as pl
from jax.experimental.pallas import tpu as pltpu
from jax.sharding import PartitionSpec as P

Q_HEADS = 64
KEY_VALUE_HEADS = 8
GROUP = Q_HEADS // KEY_VALUE_HEADS
WIDTH = 128
PIECE = 64
TILE = 2048
SCORE_SCALE = math.log2(math.e) / math.sqrt(WIDTH)
NEGATIVE = -1e30
LARGE = 1e30
NT = (((1,), (1,)), ((), ()))
f32, bf16 = jnp.float32, jnp.bfloat16


def with_ones(values):
    return jnp.concatenate([values, jnp.ones(values.shape, values.dtype)], axis=1)


def spread(column, count):
    return jnp.concatenate([column] * count, axis=1)


def flat(kv_ref, part):
    return kv_ref[:, part].reshape(kv_ref.shape[0] * kv_ref.shape[2], WIDTH)


def head_of(q_ref, head):
    return q_ref[:, head * WIDTH:(head + 1) * WIDTH]


def suffix_scores(query, keys):
    scores = lax.dot_general(query, keys, NT, preferred_element_type=f32) * SCORE_SCALE
    row = lax.broadcasted_iota(jnp.int32, scores.shape, 0)
    col = lax.broadcasted_iota(jnp.int32, scores.shape, 1)
    return jnp.where(col <= row, scores, NEGATIVE)


def add_piece(query, shift, kv_ref, total):
    keys, values = flat(kv_ref, 0), with_ones(flat(kv_ref, 1))
    wide = spread(shift, TILE // WIDTH)
    for start in range(0, keys.shape[0], TILE):
        scores = lax.dot_general(query, keys[start:start + TILE], NT, preferred_element_type=f32)
        weights = jnp.exp2(scores * SCORE_SCALE - wide).astype(bf16)
        total = total + jnp.dot(weights, values[start:start + TILE], preferred_element_type=f32)
    return total


def first_kernel(q_ref, k_ref, v_ref, kv_ref, shift_ref, total_ref):
    for head in range(GROUP):
        query = head_of(q_ref, head)
        scores = suffix_scores(query, k_ref[...])
        shift = jnp.broadcast_to(jnp.max(scores, axis=1, keepdims=True), (scores.shape[0], WIDTH))
        weights = jnp.exp2(scores - spread(shift, scores.shape[1] // WIDTH)).astype(bf16)
        total = jnp.dot(weights, with_ones(v_ref[...]), preferred_element_type=f32)
        shift_ref[head] = shift
        total_ref[head] = add_piece(query, shift, kv_ref, total)


def last_kernel(q_ref, shift_ref, total_in, kv_ref, k_ref, v_ref, other_ref, out_ref):
    worst = jnp.zeros(shift_ref.shape[1:], f32)
    for head in range(GROUP):
        total = add_piece(head_of(q_ref, head), shift_ref[head], kv_ref, total_in[head])
        weight = total[:, WIDTH:]
        worst = jnp.maximum(worst, jnp.where(weight < LARGE, 0.0, 1.0))
        out_ref[:, head * WIDTH:(head + 1) * WIDTH] = (total[:, :WIDTH] / weight).astype(bf16)

    @pl.when(jnp.max(worst) > 0.0)
    def _():
        def one_head(head, carry):
            at = pl.ds(pl.multiple_of(head * WIDTH, WIDTH), WIDTH)
            query = q_ref[:, at]

            def block(state, scores, values):
                shift, total = state
                newest = jnp.maximum(shift, jnp.max(scores, axis=1, keepdims=True))
                weights = jnp.exp2(scores - newest).astype(bf16)
                added = jnp.dot(weights, with_ones(values), preferred_element_type=f32)
                return newest, total * jnp.exp2(shift - newest) + added

            state = (jnp.full((query.shape[0], 1), NEGATIVE, f32), jnp.zeros((query.shape[0], 2 * WIDTH), f32))
            state = block(state, suffix_scores(query, k_ref[...]), v_ref[...])
            for ref in (other_ref, kv_ref):
                def step(i, state, ref=ref):
                    some = ref.at[pl.ds(i * 8, 8)]
                    scores = lax.dot_general(query, flat(some, 0), NT, preferred_element_type=f32) * SCORE_SCALE
                    return block(state, scores, flat(some, 1))

                state = lax.fori_loop(0, ref.shape[0] // 8, step, state)
            total = state[1]
            out_ref[:, at] = (total[:, :WIDTH] / total[:, WIDTH:]).astype(bf16)
            return carry

        lax.fori_loop(0, GROUP, one_head, 0)


def call(kernel, out_shape, keys, *args):
    flops = 8 * args[0].shape[0] * GROUP * keys * WIDTH
    in_vmem = pl.BlockSpec(memory_space=pltpu.VMEM)
    return pl.pallas_call(
        kernel,
        in_specs=[in_vmem] * len(args),
        out_specs=jax.tree.map(lambda _: in_vmem, out_shape),
        out_shape=out_shape,
        compiler_params=pltpu.CompilerParams(vmem_limit_bytes=24 * 1024 * 1024),
        cost_estimate=pl.CostEstimate(flops=flops, bytes_accessed=4 * 1024 * 1024, transcendentals=0),
    )(*args)


def local(owner, queries, rotated_suffix_keys, suffix_values, prefix_keys, prefix_values):
    rep, tp = lax.axis_index("rep"), lax.axis_index("tp")
    size = lax.axis_size("rep")
    rows = queries.shape[0]
    mine = owner[tp]

    def place(z, side, core):
        return 4 * z + 2 * side + core

    near = [[place(2 * a + b, s, c) for b in range(2) for s in range(2)] for a in range(8) for c in range(2)]
    far = [[place(2 * a + b, s, c) for a in range(8)] for b in range(2) for s in range(2) for c in range(2)]
    swap_core = [(i, i ^ 1) for i in range(size)]

    def exchange(array, groups):
        return lax.all_to_all(array, "rep", 0, 0, axis_index_groups=groups, tiled=True)

    def copies(array, count):
        many = jnp.broadcast_to(array[None], (count, *array.shape))
        return many.reshape(count * array.shape[0], *array.shape[1:])

    count = prefix_keys.shape[0] // 2
    half = count // PIECE
    core = rep & 1
    shape = (half, 2, PIECE, WIDTH)
    is_key = lax.broadcasted_iota(jnp.int32, shape, 1) == 0

    def half_of(which):
        at = which * count
        keys, values = (
            lax.dynamic_slice_in_dim(array, at, count, 0, allow_negative_indices=False).reshape(half, 1, PIECE, WIDTH)
            for array in (prefix_keys, prefix_values)
        )
        return jnp.where(is_key, keys, values)

    in_far = mine >> 3
    share = half // 4
    in_near = ((mine >> 1) & 3) * share
    owner_core = mine - 8 * in_far - 2 * (in_near // share)
    here = in_far == rep >> 3
    got = lax.ppermute(half_of(1 - core), "rep", swap_core)
    part = jnp.where(here & (owner_core == core), half_of(core), got)
    part = lax.dynamic_slice_in_dim(exchange(part, near), in_near, share, 0, allow_negative_indices=False)
    part = jnp.where(here, part, jnp.zeros_like(part)).astype(f32)
    part = lax.psum(part, "rep", axis_index_groups=far).astype(bf16)
    first = exchange(copies(part, 4), near)
    second = lax.ppermute(first, "rep", swap_core)

    shift_shape = jax.ShapeDtypeStruct((GROUP, rows, WIDTH), f32)
    total_shape = jax.ShapeDtypeStruct((GROUP, rows, 2 * WIDTH), f32)
    suffix = (rotated_suffix_keys, suffix_values)
    shift, total = call(first_kernel, (shift_shape, total_shape), rows + half * PIECE, queries, *suffix, first)
    output = call(
        last_kernel, jax.ShapeDtypeStruct(queries.shape, bf16), half * PIECE,
        queries, shift, total, second, *suffix, first,
    )
    return lax.all_to_all(output, "tp", split_axis=0, concat_axis=1, tiled=True)


def solution(mesh):
    in_specs = (P(), P("rep", "tp"), P("rep", "tp"), P("rep", "tp"), P("rep", "tp"), P("rep", "tp"))
    out_specs = P(("rep", "tp"), None)
    return jax.shard_map(local, mesh=mesh, in_specs=in_specs, out_specs=out_specs, check_vma=False)
```
